32 devices in a mesh: engine: 8 (over y, x, core), tensor: 4 (over z).
Axes of the slice: x: 2, y: 2, z: 4, core: 2. Of those that a mesh axis runs over, the one named last changes fastest.
Arguments:
- hidden: bfloat16 [4096, 5120], P('engine'), may hold values from -6 to 6
- lengths: int32 [16], replicated, may hold values from 1 to 256, as said below
- assignment: int32 [16], replicated, may hold values from 0 to 7, as said below
- wq: bfloat16 [2, 5120, 4096], P(None, ('engine', 'tensor')), may hold values from -0.078125 to 0.078125
- wkv: bfloat16 [2, 5120, 2048], P(None, ('engine', 'tensor')), may hold values from -0.078125 to 0.078125
- wo: bfloat16 [2, 4096, 5120], P(None, None, ('engine', 'tensor')), may hold values from -0.5 to 0.5
- norm_gain: float32 [2, 5120], replicated, may hold values from 0.5 to 1.5
- qk_gain: float32 [2, 2, 128], replicated, may hold values from 0.5 to 1.5
Outputs:
- new_hidden: bfloat16 [4096, 5120], P('engine')
- kv_cache: bfloat16 [2, 4096, 2048], P(None, 'engine', 'tensor')
The draws below stay inside these ranges and needn't reach their ends.
Inputs may be any that keep to these rules, and one draw needn't show every extreme that they name: `lengths`: each rollout has 1 to 256 tokens; in every draw all rollouts of some engine have exactly 256. `assignment`: every engine is named by exactly 2 rollouts, so an engine's rollouts fill at most its 512 rows, and some engine's fill all of them.
All inputs are finite; a program needn't handle non-finite values.
Results may differ from the reference program's by a relative error of at most 0.018.
Values may be sent and summed in bfloat16 or wider, within the bound.
A program may use at most 128 MiB of HBM per device.

```python
import jax
import jax.numpy as jnp
from jax import lax

D = 5120
HQ = 32
KVH = 8
HD = 128
LAYERS = 2
SLOTS = 2
MAXLEN = 256
CAP = 512
SEQS = 16
ROWS = 4096
N_ENGINE = 8
N_TENSOR = 4


def rollout_layout(key):
    keys = jax.random.split(key, 4)
    shuffled = jax.random.permutation(keys[0], SEQS).astype(jnp.int32)
    assignment = (shuffled // SLOTS).astype(jnp.int32)
    first_draw = jax.random.randint(keys[1], (SEQS,), 0, MAXLEN)
    second_draw = jax.random.randint(keys[2], (SEQS,), 0, MAXLEN)
    raw_lengths = 1 + jnp.maximum(first_draw, second_draw)
    busiest = jax.random.randint(keys[3], (), 0, SEQS // SLOTS)
    lengths = jnp.where(assignment == busiest, MAXLEN, raw_lengths).astype(jnp.int32)
    return (assignment, lengths)


def draw_lengths(key, part):
    assignment, lengths = rollout_layout(key)
    return lengths


def draw_assignment(key, part):
    assignment, lengths = rollout_layout(key)
    return assignment


def draw_hidden(key, part):
    key = jax.random.fold_in(key, 7)
    keys = jax.random.split(key, 3)
    base = jax.random.truncated_normal(keys[0], -4.0, 4.0, (ROWS, D), jnp.float32)
    row_scale = jnp.exp(jax.random.uniform(keys[1], (ROWS, 1), jnp.float32, jnp.log(0.1), 0.0))
    col_scale = jnp.exp(jax.random.uniform(keys[2], (1, D), jnp.float32, jnp.log(0.3), jnp.log(3.0)))
    return (0.5 * base * row_scale * col_scale).astype(jnp.bfloat16)


def steps_of(rng, extent, cuts, least, high):
    factor_of, own = 1.0, jax.random.fold_in(rng, 6)
    for dim, shards_of in cuts:
        draws = jnp.exp(jax.random.uniform(jax.random.fold_in(own, dim), (shards_of,), jnp.float32, least / len(cuts), high / len(cuts)))
        factor_of = factor_of * jnp.repeat(draws, extent[dim] // shards_of).reshape([-1 if axis == dim else 1 for axis in range(len(extent))])
    return factor_of


def noise(stream_key, dims, width, most, cuts=(), kind=jnp.bfloat16):
    array = width * jax.random.normal(stream_key, dims, jnp.float32)
    if cuts:
        array = array * steps_of(stream_key, dims, cuts, -0.22, 0.18)
    return jnp.clip(array, -most, most).astype(kind)


def setup_inputs(seed: int = 0) -> dict:
    key_of = jax.random.split(jax.random.key(seed), 9)
    return {
        "hidden": draw_hidden(jax.random.fold_in(key_of[8], 71), 0),
        "lengths": draw_lengths(jax.random.fold_in(key_of[8], 71), 0),
        "assignment": draw_assignment(jax.random.fold_in(key_of[8], 71), 0),
        "wq": noise(key_of[3], (LAYERS, D, HQ * HD), D ** -0.5, 0.078125, ((1, 32),)),
        "wkv": noise(key_of[4], (LAYERS, D, KVH * 2 * HD), D ** -0.5, 0.078125, ((1, 32),)),
        "wo": noise(key_of[5], (LAYERS, HQ * HD, D), HD ** -0.5, 0.5, ((2, 32),)),
        "norm_gain": jnp.clip(1.0 + 0.1 * jax.random.normal(key_of[6], (LAYERS, D), jnp.float32), 0.5, 1.5),
        "qk_gain": jnp.clip(1.0 + 0.1 * jax.random.normal(key_of[7], (LAYERS, 2, HD), jnp.float32), 0.5, 1.5),
    }


EPS = 1e-06
THETA = 1000000.0

def row_layout(lengths, assignment, engine, row_count):
    on_engine = assignment == engine
    own_sizes = jnp.where(on_engine, lengths, 0).astype(jnp.int32)
    offsets = (jnp.cumsum(own_sizes) - own_sizes).astype(jnp.int32)
    row_ids = jnp.arange(row_count, dtype=jnp.int32)
    inside = on_engine[None, :] & (row_ids[:, None] >= offsets[None, :]) & (row_ids[:, None] < (offsets + own_sizes)[None, :])
    inside_int = inside.astype(jnp.int32)
    seq_index = jnp.arange(lengths.shape[0], dtype=jnp.int32)
    live_count = lax.optimization_barrier(jnp.sum(inside_int, axis=1))
    segment = lax.optimization_barrier(jnp.sum(inside_int * seq_index[None, :], axis=1)).astype(jnp.int32)
    segment = jnp.where(live_count > 0, segment, lengths.shape[0] + row_ids).astype(jnp.int32)
    position = row_ids - lax.optimization_barrier(jnp.sum(inside_int * offsets[None, :], axis=1)).astype(jnp.int32)
    position = jnp.where(live_count > 0, position, 0).astype(jnp.int32)
    return (segment, position)

def rope_tables(position, head_size):
    half_width = head_size // 2
    frequency = jnp.power(jnp.float32(THETA), -(jnp.arange(half_width, dtype=jnp.float32) * 2.0 / head_size))
    angles = position.astype(jnp.float32)[:, None] * frequency[None, :]
    return (jnp.cos(angles)[:, None, :], jnp.sin(angles)[:, None, :])

def rotate(values, cosine, sine_part):
    half_width = values.shape[-1] // 2
    first_half = values[..., :half_width]
    second_half = values[..., half_width:]
    return jnp.concatenate([first_half * cosine - second_half * sine_part, second_half * cosine + first_half * sine_part], axis=-1)

def head_norm(values, gain_row):
    return values * lax.rsqrt(lax.optimization_barrier(jnp.mean(values * values, axis=-1, keepdims=True)) + EPS) * gain_row

def norm_rows(values, gain_row):
    widened = values.astype(jnp.float32)
    return (widened * lax.rsqrt(lax.optimization_barrier(jnp.mean(widened * widened, axis=-1, keepdims=True)) + EPS) * gain_row).astype(jnp.bfloat16)

def attend(queries, key_heads, value_heads, segment):
    row_count = queries.shape[0]
    scores = jnp.einsum('rkgd,ckd->kgrc', queries.astype(jnp.float32), key_heads.astype(jnp.float32)) * queries.shape[-1] ** (-0.5)
    row_ids = jnp.arange(row_count, dtype=jnp.int32)
    allowed = (segment[:, None] == segment[None, :]) & (row_ids[None, :] <= row_ids[:, None])
    raised = jnp.exp(scores) * allowed.astype(jnp.float32)
    weights = (raised / lax.optimization_barrier(jnp.sum(raised, axis=-1, keepdims=True))).astype(jnp.bfloat16)
    attended = jnp.einsum('kgrc,ckd->rkgd', weights.astype(jnp.float32), value_heads.astype(jnp.float32))
    return attended.astype(jnp.bfloat16).reshape(row_count, -1)

def engine_pass(state, segment, position, wq, wkv, wo, norm_gain, qk_gain):
    row_count = state.shape[0]
    cosine, sine_part = rope_tables(position, HD)
    caches = []
    for layer_number in range(LAYERS):
        widened = state.astype(jnp.float32)
        normed = norm_rows(state, norm_gain[layer_number])
        queries = jnp.dot(normed, wq[layer_number], preferred_element_type=jnp.float32).reshape(row_count, HQ, HD)
        keyvals = jnp.dot(normed, wkv[layer_number], preferred_element_type=jnp.float32).reshape(row_count, KVH, 2, HD)
        queries = rotate(head_norm(queries, qk_gain[layer_number, 0]), cosine, sine_part).astype(jnp.bfloat16)
        key_heads = rotate(head_norm(keyvals[:, :, 0], qk_gain[layer_number, 1]), cosine, sine_part).astype(jnp.bfloat16)
        value_heads = keyvals[:, :, 1].astype(jnp.bfloat16)
        caches.append(jnp.stack([key_heads, value_heads], axis=2).reshape(row_count, KVH * 2 * HD))
        attended = attend(queries.reshape(row_count, KVH, HQ // KVH, HD), key_heads, value_heads, segment)
        group_width = HQ * HD // N_TENSOR
        summed = jnp.zeros((row_count, D), jnp.float32)
        for group_number in range(N_TENSOR):
            term = jnp.dot(attended[:, group_number * group_width:(group_number + 1) * group_width], wo[layer_number, group_number * group_width:(group_number + 1) * group_width], preferred_element_type=jnp.float32)
            summed = summed + lax.optimization_barrier(term.astype(jnp.bfloat16)).astype(jnp.float32)
        state = (widened + summed).astype(jnp.bfloat16)
    return (state, jnp.stack(caches))

def reference(hidden, lengths, assignment, wq, wkv, wo, norm_gain, qk_gain):
    blocks = hidden.reshape(N_ENGINE, CAP, D)

    def per_engine(engine_args):
        engine_block, engine = engine_args
        segment, position = row_layout(lengths, assignment, engine, CAP)
        return engine_pass(engine_block, segment, position, wq, wkv, wo, norm_gain, qk_gain)
    states, caches = lax.map(per_engine, (blocks, jnp.arange(N_ENGINE, dtype=jnp.int32)))
    new_hidden = states.reshape(N_ENGINE * CAP, D)
    kv_cache = jnp.transpose(caches, (1, 0, 2, 3)).reshape(LAYERS, N_ENGINE * CAP, KVH * 2 * HD)
    return (new_hidden, kv_cache)
```

```python
import functools

import jax
import jax.numpy as jnp
from jax import lax
from jax.experimental import pallas as pl
from jax.experimental.pallas import tpu as pltpu
from jax.sharding import PartitionSpec as P

EPS = 1e-06
THETA = 1000000.0


def row_layout(lengths, assignment, engine, row_count):
    on_engine = assignment == engine
    own_sizes = jnp.where(on_engine, lengths, 0)
    offsets = jnp.cumsum(own_sizes) - own_sizes
    row_ids = jnp.arange(row_count, dtype=jnp.int32)
    inside = (
        on_engine[None, :]
        & (row_ids[:, None] >= offsets[None, :])
        & (row_ids[:, None] < (offsets + own_sizes)[None, :])
    )
    inside_int = inside.astype(jnp.int32)
    seq_index = jnp.arange(lengths.shape[0], dtype=jnp.int32)
    live_count = jnp.sum(inside_int, axis=1)
    segment = jnp.sum(inside_int * seq_index[None, :], axis=1)
    segment = jnp.where(live_count > 0, segment, lengths.shape[0] + row_ids)
    position = row_ids - jnp.sum(inside_int * offsets[None, :], axis=1)
    position = jnp.where(live_count > 0, position, 0)
    return (segment, position)


def rope_tables(position, head_size):
    half_width = head_size // 2
    frequency = jnp.power(
        jnp.float32(THETA), -(jnp.arange(half_width, dtype=jnp.float32) * 2.0 / head_size)
    )
    angles = position.astype(jnp.float32)[:, None] * frequency[None, :]
    return (jnp.cos(angles)[:, None, :], jnp.sin(angles)[:, None, :])


def rotate(values, cosine, sine_part):
    half_width = values.shape[-1] // 2
    first_half = values[..., :half_width]
    second_half = values[..., half_width:]
    return jnp.concatenate(
        [
            first_half * cosine - second_half * sine_part,
            second_half * cosine + first_half * sine_part,
        ],
        axis=-1,
    )


def head_norm(values, gain_row):
    return values * lax.rsqrt(jnp.mean(values * values, axis=-1, keepdims=True) + EPS) * gain_row


def norm_rows(values, gain_row):
    widened = values.astype(jnp.float32)
    return (
        widened * lax.rsqrt(jnp.mean(widened * widened, axis=-1, keepdims=True) + EPS) * gain_row
    ).astype(jnp.bfloat16)


def attend(queries, key_heads, value_heads, segment):
    row_count = queries.shape[0]
    scores = jnp.einsum(
        "rkgd,ckd->kgrc", queries, key_heads, preferred_element_type=jnp.float32
    ) * queries.shape[-1] ** (-0.5)
    row_ids = jnp.arange(row_count, dtype=jnp.int32)
    allowed = (segment[:, None] == segment[None, :]) & (row_ids[None, :] <= row_ids[:, None])
    raised = jnp.exp(scores) * allowed.astype(jnp.float32)
    weights = (raised / jnp.sum(raised, axis=-1, keepdims=True)).astype(jnp.bfloat16)
    attended = jnp.einsum(
        "kgrc,ckd->rkgd", weights, value_heads, preferred_element_type=jnp.float32
    )
    return attended.astype(jnp.bfloat16).reshape(row_count, -1)


def shards(hidden, lengths, assignment, wq, wkv, wo, norm_gain, qk_gain):
    row_count = hidden.shape[0]
    tensor_size = lax.axis_size("tensor")
    head_size = qk_gain.shape[-1]
    layer_total = wq.shape[0]
    local_queries = wq.shape[2] // tensor_size // head_size
    local_keys = wkv.shape[2] // tensor_size // (2 * head_size)
    segment, position = row_layout(lengths, assignment, lax.axis_index("engine"), row_count)
    cosine, sine_part = rope_tables(position, head_size)
    residual = hidden
    normed = norm_rows(hidden, norm_gain[0])
    caches = []
    for layer_number in range(layer_total):
        if layer_number > 0:
            normed = norm_rows(residual, norm_gain[layer_number])
        query_part, keyval_part = (
            lax.all_to_all(wq[layer_number], "tensor", split_axis=1, concat_axis=0, tiled=True),
            lax.all_to_all(wkv[layer_number], "tensor", split_axis=1, concat_axis=0, tiled=True),
        )
        query_weight, keyval_weight = (
            lax.all_gather(query_part, "engine", axis=0, tiled=True),
            lax.all_gather(keyval_part, "engine", axis=0, tiled=True),
        )
        queries = jnp.dot(normed, query_weight, preferred_element_type=jnp.float32)
        keyvals = jnp.dot(normed, keyval_weight, preferred_element_type=jnp.float32)
        queries = queries.reshape(row_count, local_queries, head_size)
        keyvals = keyvals.reshape(row_count, local_keys, 2, head_size)
        queries = rotate(head_norm(queries, qk_gain[layer_number, 0]), cosine, sine_part).astype(
            jnp.bfloat16
        )
        key_heads = rotate(
            head_norm(keyvals[:, :, 0], qk_gain[layer_number, 1]), cosine, sine_part
        ).astype(jnp.bfloat16)
        value_heads = keyvals[:, :, 1].astype(jnp.bfloat16)
        caches.append(
            jnp.stack([key_heads, value_heads], axis=2).reshape(
                row_count, local_keys * 2 * head_size
            )
        )
        attended = attend(
            queries.reshape(row_count, local_keys, local_queries // local_keys, head_size),
            key_heads,
            value_heads,
            segment,
        )
        out_part = lax.all_to_all(
            wo[layer_number], "tensor", split_axis=0, concat_axis=1, tiled=True
        )
        out_weight = lax.all_gather(out_part, "engine", axis=1, tiled=True)
        partial_term = jnp.dot(attended, out_weight, preferred_element_type=jnp.float32)
        summed = lax.psum(partial_term.astype(jnp.bfloat16), "tensor").astype(jnp.float32)
        residual = (residual.astype(jnp.float32) + summed).astype(jnp.bfloat16)
    return (residual, jnp.stack(caches))


MESH = pl.DeviceIdType.MESH
ENGINES, TENSORS = 8, 4
SUM_CHUNKS = 16


def comm_kernel(n_gather, with_sum, *refs):
    refs = list(refs)
    ins = [refs.pop(0) for _ in range(n_gather)]
    if with_sum:
        term, resid = refs.pop(0), refs.pop(0)
    outs = [refs.pop(0) for _ in range(n_gather)]
    if with_sum:
        total = refs.pop(0)
    if n_gather:
        own_sem, zs, zr, ps, pr, ds, dr, cs, cr = refs[:9]
        refs = refs[9:]
    if with_sum:
        got_end, mine, got_mid, e_send, e_recv, m_send, m_recv, o_send, o_recv = refs

    e, t = lax.axis_index("engine"), lax.axis_index("tensor")
    core, xb, yb = e % 2, (e // 2) % 2, e // 4
    sib, xn, yn = e + 1 - 2 * core, e + 2 - 4 * xb, e + 4 - 8 * yb
    dg = xn + yn - e

    barrier = pltpu.get_barrier_semaphore()
    partners = [(e, (t + k) % TENSORS) for k in range(1, TENSORS)]
    if n_gather:
        partners += [(sib, t), (xn, t), (yn, t)]
    for dev in partners:
        pl.semaphore_signal(barrier, inc=1, device_id=dev, device_id_type=MESH)
    pl.semaphore_wait(barrier, len(partners))

    def rc(src, dst, ss, rs, dev):
        return pltpu.make_async_remote_copy(
            src_ref=src, dst_ref=dst, send_sem=ss, recv_sem=rs, device_id=dev, device_id_type=MESH
        )

    if n_gather:
        rows = ins[0].shape[1]
        half = rows // 2

    def slot(k):
        return (t + TENSORS - k) % TENSORS

    def z_out(i, k):
        to = (t + k) % TENSORS
        return rc(ins[i].at[to], outs[i].at[e, t], zs.at[i, k - 1], zr.at[i, k - 1], (e, to))

    def z_in(i, k):
        here = outs[i].at[e, slot(k)]
        return rc(here, here, zs.at[i, k - 1], zr.at[i, k - 1], (e, slot(k)))

    def own(i):
        return pltpu.make_async_copy(ins[i].at[t], outs[i].at[e, t], own_sem.at[i])

    def plane(i, k, src, which):
        there = outs[i].at[src, slot(k)]
        source = ins[i].at[t] if k == 0 and src is e else there
        dev = ((xn, t), (yn, t))[which]
        return rc(source, there, ps.at[i, k, which], pr.at[i, k, which], dev)

    def diag(i, k, src, which):
        there = outs[i].at[src, slot(k), pl.ds(which * half, half)]
        dev = ((yn, t), (xn, t))[which]
        return rc(there, there, ds.at[i, k, which], dr.at[i, k, which], dev)

    def cross(i, k, src, which):
        there = outs[i].at[src, slot(k)]
        source = ins[i].at[t] if k == 0 and which == 0 and src is e else there
        return rc(source, there, cs.at[i, k, which], cr.at[i, k, which], (sib, t))

    def stage0(i, k):
        if k > 0:
            z_in(i, k).wait_recv()
        plane(i, k, e, 0).start()
        plane(i, k, e, 1).start()
        cross(i, k, e, 0).start()

    def stage1(i, k):
        plane(i, k, xn, 0).wait_recv()
        diag(i, k, xn, 0).start()
        cross(i, k, xn, 1).start()
        plane(i, k, yn, 1).wait_recv()
        diag(i, k, yn, 1).start()
        cross(i, k, yn, 2).start()

    def stage2(i, k):
        diag(i, k, dg, 0).wait_recv()
        diag(i, k, dg, 1).wait_recv()
        cross(i, k, dg, 3).start()

    def stage3(i, k):
        sx, sy = xn + sib - e, yn + sib - e
        for which, src in enumerate((sib, sx, sy, sx + sy - sib)):
            cross(i, k, src, which).wait_recv()
        if k > 0:
            z_out(i, k).wait_send()
        else:
            own(i).wait()
        plane(i, k, e, 0).wait_send()
        plane(i, k, e, 1).wait_send()
        diag(i, k, xn, 0).wait_send()
        diag(i, k, yn, 1).wait_send()
        for which, src in enumerate((e, xn, yn, dg)):
            cross(i, k, src, which).wait_send()

    is_end = (t == 0) | (t == TENSORS - 1)
    end_peer = jnp.where(t < 2, 1 - t, 5 - t)
    mid_peer = 3 - t

    def band(ref, c):
        size = ref.shape[0] // SUM_CHUNKS
        return ref.at[pl.ds(c * size, size)]

    def end_copy(c):
        return rc(band(term, c), band(got_end, c), e_send.at[c], e_recv.at[c], (e, end_peer))

    def mid_copy(c):
        return rc(band(mine, c), band(got_mid, c), m_send.at[c], m_recv.at[c], (e, mid_peer))

    def out_copy(c):
        return rc(band(total, c), band(total, c), o_send.at[c], o_recv.at[c], (e, end_peer))

    def sum_first(c):
        @pl.when(jnp.logical_not(is_end))
        def _():
            end_copy(c).wait_recv()
            band(mine, c)[...] = (
                band(term, c)[...].astype(jnp.float32) + band(got_end, c)[...].astype(jnp.float32)
            ).astype(jnp.bfloat16)
            mid_copy(c).start()

    def sum_second(c):
        @pl.when(jnp.logical_not(is_end))
        def _():
            mid_copy(c).wait_recv()
            both = band(mine, c)[...].astype(jnp.float32) + band(got_mid, c)[...].astype(jnp.float32)
            band(total, c)[...] = (band(resid, c)[...].astype(jnp.float32) + both).astype(
                jnp.bfloat16
            )
            out_copy(c).start()

    if with_sum:

        @pl.when(is_end)
        def _():
            @pl.loop(0, SUM_CHUNKS)
            def _(c):
                end_copy(c).start()

    order = [(i, k) for i in range(n_gather) for k in range(TENSORS)]
    for i in range(n_gather):
        own(i).start()
    for i in range(n_gather):
        for k in range(1, TENSORS):
            z_out(i, k).start()
    steps = len(order) + 3 if n_gather else SUM_CHUNKS + 2
    per_step = -(-(SUM_CHUNKS + 2) // max(1, len(order))) if n_gather else 1
    done = 0
    if with_sum and not n_gather:
        sum_first(0)
        sum_first(1)

        @pl.loop(2, SUM_CHUNKS)
        def _(c):
            sum_first(c)
            sum_second(c - 2)

        sum_second(SUM_CHUNKS - 2)
        sum_second(SUM_CHUNKS - 1)
    if n_gather:
        for step in range(steps):
            if step < len(order):
                stage0(*order[step])
            if with_sum:
                for _ in range(per_step):
                    if done < SUM_CHUNKS:
                        sum_first(done)
                    if 2 <= done < SUM_CHUNKS + 2:
                        sum_second(done - 2)
                    done += 1
            if 0 <= step - 1 < len(order):
                stage1(*order[step - 1])
            if 0 <= step - 2 < len(order):
                stage2(*order[step - 2])
        for item in order:
            stage3(*item)
    if with_sum:

        @pl.when(is_end)
        def _():
            @pl.loop(0, SUM_CHUNKS)
            def _(c):
                out_copy(c).wait_recv()
                end_copy(c).wait_send()

        @pl.when(jnp.logical_not(is_end))
        def _():
            @pl.loop(0, SUM_CHUNKS)
            def _(c):
                mid_copy(c).wait_send()
                out_copy(c).wait_send()


def communicate(weights, sums, collective_id):
    n = len(weights)
    outs = [jax.ShapeDtypeStruct((ENGINES,) + w.shape, w.dtype) for w in weights]
    in_specs = [pl.BlockSpec(memory_space=pl.ANY)] * n
    out_specs = [pl.BlockSpec(memory_space=pl.ANY)] * n
    scratch = []
    dma = pltpu.SemaphoreType.DMA
    if n:
        scratch += [dma((n,)), dma((n, 3)), dma((n, 3))]
        scratch += [dma((n, 4, 2))] * 4 + [dma((n, 4, 4))] * 2
    if sums:
        in_specs += [pl.BlockSpec(memory_space=pltpu.VMEM)] * 2
        outs.append(jax.ShapeDtypeStruct(sums[0].shape, jnp.bfloat16))
        out_specs.append(pl.BlockSpec(memory_space=pltpu.VMEM))
        scratch += [pltpu.VMEM(sums[0].shape, jnp.bfloat16)] * 3
        scratch += [dma((SUM_CHUNKS,))] * 6
    return pl.pallas_call(
        functools.partial(comm_kernel, n, bool(sums)),
        out_shape=outs,
        in_specs=in_specs,
        out_specs=out_specs,
        scratch_shapes=scratch,
        compiler_params=pltpu.CompilerParams(
            collective_id=collective_id, has_side_effects=True, vmem_limit_bytes=44 * 1024 * 1024
        ),
        cost_estimate=pl.CostEstimate(flops=0, bytes_accessed=60_000_000, transcendentals=0),
    )(*weights, *sums)


def fast_shards(hidden, lengths, assignment, wq, wkv, wo, norm_gain, qk_gain):
    row_count, width = hidden.shape
    head_size = qk_gain.shape[-1]
    layer_total, depth = wq.shape[0], wq.shape[1]
    q_width, kv_width = wq.shape[2] // TENSORS, wkv.shape[2] // TENSORS
    local_queries, local_keys = q_width // head_size, kv_width // (2 * head_size)
    segment, position = row_layout(lengths, assignment, lax.axis_index("engine"), row_count)
    cosine, sine_part = rope_tables(position, head_size)

    def by_target(layer_number):
        queries = wq[layer_number].reshape(depth, TENSORS, q_width)
        keyvals = wkv[layer_number].reshape(depth, TENSORS, kv_width)
        both = jnp.concatenate([queries, keyvals], axis=2).transpose(1, 0, 2)
        out = wo[layer_number].reshape(TENSORS, q_width, depth).transpose(0, 2, 1)
        return [both, out]

    residual = hidden
    caches = []
    weights = communicate(by_target(0), [], 1)
    for layer_number in range(layer_total):
        normed = norm_rows(residual, norm_gain[layer_number])
        qkv_weight = weights[0].reshape(width, q_width + kv_width)
        out_weight = weights[1].reshape(width, q_width)
        projected = jnp.dot(normed, qkv_weight, preferred_element_type=jnp.float32)
        queries = projected[:, :q_width].reshape(row_count, local_queries, head_size)
        keyvals = projected[:, q_width:].reshape(row_count, local_keys, 2, head_size)
        queries = rotate(head_norm(queries, qk_gain[layer_number, 0]), cosine, sine_part).astype(
            jnp.bfloat16
        )
        key_heads = rotate(
            head_norm(keyvals[:, :, 0], qk_gain[layer_number, 1]), cosine, sine_part
        ).astype(jnp.bfloat16)
        value_heads = keyvals[:, :, 1].astype(jnp.bfloat16)
        caches.append(
            jnp.stack([key_heads, value_heads], axis=2).reshape(
                row_count, local_keys * 2 * head_size
            )
        )
        attended = attend(
            queries.reshape(row_count, local_keys, local_queries // local_keys, head_size),
            key_heads,
            value_heads,
            segment,
        )
        term = lax.dot_general(
            attended, out_weight, (((1,), (1,)), ((), ())), preferred_element_type=jnp.float32
        ).astype(jnp.bfloat16)
        if layer_number + 1 < layer_total:
            *weights, residual = communicate(
                by_target(layer_number + 1), [term, residual], 2 + layer_number
            )
        else:
            (residual,) = communicate([], [term, residual], 2 + layer_number)
    return (residual, jnp.stack(caches))


def solution(mesh):
    fits = mesh.shape["engine"] == ENGINES and mesh.shape["tensor"] == TENSORS
    return jax.shard_map(
        fast_shards if fits else shards,
        mesh=mesh,
        in_specs=(
            P("engine", None),
            P(),
            P(),
            P(None, ("engine", "tensor"), None),
            P(None, ("engine", "tensor"), None),
            P(None, None, ("engine", "tensor")),
            P(),
            P(),
        ),
        out_specs=(P("engine", None), P(None, "engine", "tensor")),
        check_vma=False,
    )
```

```python
import functools

import jax
import jax.numpy as jnp
from jax import lax
from jax.experimental import pallas as pl
from jax.experimental.pallas import tpu as pltpu
from jax.sharding import PartitionSpec as P

EPS = 1e-06
THETA = 1000000.0


def row_layout(lengths, assignment, engine, row_count):
    on_engine = assignment == engine
    own_sizes = jnp.where(on_engine, lengths, 0)
    offsets = jnp.cumsum(own_sizes) - own_sizes
    row_ids = jnp.arange(row_count, dtype=jnp.int32)
    inside = (
        on_engine[None, :]
        & (row_ids[:, None] >= offsets[None, :])
        & (row_ids[:, None] < (offsets + own_sizes)[None, :])
    )
    inside_int = inside.astype(jnp.int32)
    seq_index = jnp.arange(lengths.shape[0], dtype=jnp.int32)
    live_count = jnp.sum(inside_int, axis=1)
    segment = jnp.sum(inside_int * seq_index[None, :], axis=1)
    segment = jnp.where(live_count > 0, segment, lengths.shape[0] + row_ids)
    position = row_ids - jnp.sum(inside_int * offsets[None, :], axis=1)
    position = jnp.where(live_count > 0, position, 0)
    return (segment, position)


def rope_tables(position, head_size):
    half_width = head_size // 2
    frequency = jnp.power(
        jnp.float32(THETA), -(jnp.arange(half_width, dtype=jnp.float32) * 2.0 / head_size)
    )
    angles = position.astype(jnp.float32)[:, None] * frequency[None, :]
    return (jnp.cos(angles)[:, None, :], jnp.sin(angles)[:, None, :])


def rotate(values, cosine, sine_part):
    half_width = values.shape[-1] // 2
    first_half = values[..., :half_width]
    second_half = values[..., half_width:]
    return jnp.concatenate(
        [
            first_half * cosine - second_half * sine_part,
            second_half * cosine + first_half * sine_part,
        ],
        axis=-1,
    )


def head_norm(values, gain_row):
    return values * lax.rsqrt(jnp.mean(values * values, axis=-1, keepdims=True) + EPS) * gain_row


def norm_rows(values, gain_row):
    widened = values.astype(jnp.float32)
    return (
        widened * lax.rsqrt(jnp.mean(widened * widened, axis=-1, keepdims=True) + EPS) * gain_row
    ).astype(jnp.bfloat16)


def attend(queries, key_heads, value_heads, segment):
    row_count = queries.shape[0]
    scores = jnp.einsum(
        "rkgd,ckd->kgrc", queries, key_heads, preferred_element_type=jnp.float32
    ) * queries.shape[-1] ** (-0.5)
    row_ids = jnp.arange(row_count, dtype=jnp.int32)
    allowed = (segment[:, None] == segment[None, :]) & (row_ids[None, :] <= row_ids[:, None])
    raised = jnp.exp(scores) * allowed.astype(jnp.float32)
    weights = (raised / jnp.sum(raised, axis=-1, keepdims=True)).astype(jnp.bfloat16)
    attended = jnp.einsum(
        "kgrc,ckd->rkgd", weights, value_heads, preferred_element_type=jnp.float32
    )
    return attended.astype(jnp.bfloat16).reshape(row_count, -1)


def shards(hidden, lengths, assignment, wq, wkv, wo, norm_gain, qk_gain):
    row_count = hidden.shape[0]
    tensor_size = lax.axis_size("tensor")
    head_size = qk_gain.shape[-1]
    layer_total = wq.shape[0]
    local_queries = wq.shape[2] // tensor_size // head_size
    local_keys = wkv.shape[2] // tensor_size // (2 * head_size)
    segment, position = row_layout(lengths, assignment, lax.axis_index("engine"), row_count)
    cosine, sine_part = rope_tables(position, head_size)
    residual = hidden
    normed = norm_rows(hidden, norm_gain[0])
    caches = []
    for layer_number in range(layer_total):
        if layer_number > 0:
            normed = norm_rows(residual, norm_gain[layer_number])
        query_part, keyval_part = (
            lax.all_to_all(wq[layer_number], "tensor", split_axis=1, concat_axis=0, tiled=True),
            lax.all_to_all(wkv[layer_number], "tensor", split_axis=1, concat_axis=0, tiled=True),
        )
        query_weight, keyval_weight = (
            lax.all_gather(query_part, "engine", axis=0, tiled=True),
            lax.all_gather(keyval_part, "engine", axis=0, tiled=True),
        )
        queries = jnp.dot(normed, query_weight, preferred_element_type=jnp.float32)
        keyvals = jnp.dot(normed, keyval_weight, preferred_element_type=jnp.float32)
        queries = queries.reshape(row_count, local_queries, head_size)
        keyvals = keyvals.reshape(row_count, local_keys, 2, head_size)
        queries = rotate(head_norm(queries, qk_gain[layer_number, 0]), cosine, sine_part).astype(
            jnp.bfloat16
        )
        key_heads = rotate(
            head_norm(keyvals[:, :, 0], qk_gain[layer_number, 1]), cosine, sine_part
        ).astype(jnp.bfloat16)
        value_heads = keyvals[:, :, 1].astype(jnp.bfloat16)
        caches.append(
            jnp.stack([key_heads, value_heads], axis=2).reshape(
                row_count, local_keys * 2 * head_size
            )
        )
        attended = attend(
            queries.reshape(row_count, local_keys, local_queries // local_keys, head_size),
            key_heads,
            value_heads,
            segment,
        )
        out_part = lax.all_to_all(
            wo[layer_number], "tensor", split_axis=0, concat_axis=1, tiled=True
        )
        out_weight = lax.all_gather(out_part, "engine", axis=1, tiled=True)
        partial_term = jnp.dot(attended, out_weight, preferred_element_type=jnp.float32)
        summed = lax.psum(partial_term.astype(jnp.bfloat16), "tensor").astype(jnp.float32)
        residual = (residual.astype(jnp.float32) + summed).astype(jnp.bfloat16)
    return (residual, jnp.stack(caches))


MESH = pl.DeviceIdType.MESH
ENGINES, TENSORS = 8, 4
SUM_CHUNKS, WINDOW, LAG = 32, 6, 2


def comm_kernel(parts, n_outs, with_sum, *refs):
    refs = list(refs)
    first = len(parts) > 0
    n_in = len(parts) if first else n_outs
    ins = [refs.pop(0) for _ in range(n_in)]
    if with_sum:
        term, resid = refs.pop(0), refs.pop(0)
    outs = [refs.pop(0) for _ in range(n_outs)]
    if first:
        staged = [refs.pop(0) for _ in range(n_outs)]
    if with_sum:
        total = refs.pop(0)
    if n_outs:
        own_sem, ps, pr, ds, dr, cs, cr = refs[:7]
        refs = refs[7:]
    if first:
        zs, zr = refs[:2]
        refs = refs[2:]
    if with_sum:
        got_end, mine, got_mid, e_send, e_recv, m_send, m_recv, o_send, o_recv = refs

    e, t = lax.axis_index("engine"), lax.axis_index("tensor")
    core, xb, yb = e % 2, (e // 2) % 2, e // 4
    sib, xn, yn = e + 1 - 2 * core, e + 2 - 4 * xb, e + 4 - 8 * yb
    dg = xn + yn - e

    barrier = pltpu.get_barrier_semaphore()
    partners = [(e, (t + k) % TENSORS) for k in range(1, TENSORS)]
    if n_outs:
        partners += [(sib, t), (xn, t), (yn, t)]
    for dev in partners:
        pl.semaphore_signal(barrier, inc=1, device_id=dev, device_id_type=MESH)
    pl.semaphore_wait(barrier, len(partners))

    def rc(src, dst, ss, rs, dev):
        return pltpu.make_async_remote_copy(
            src_ref=src, dst_ref=dst, send_sem=ss, recv_sem=rs, device_id=dev, device_id_type=MESH
        )

    def slot(k):
        return (t + TENSORS - k) % TENSORS

    def landing(layer, p, source):
        out, column, size = parts[p]
        ref = outs[out].at[e, source] if layer == 0 else staged[out].at[source]
        return ref.at[:, pl.ds(column, size)]

    def cut(layer, p, target):
        size = parts[p][2]
        return ins[p].at[layer, :, pl.ds(pl.multiple_of(target * size, 128), size)]

    def z_out(layer, p, k):
        to = (t + k) % TENSORS
        sems = (zs.at[layer, p, k - 1], zr.at[layer, p, k - 1])
        return rc(cut(layer, p, to), landing(layer, p, t), *sems, (e, to))

    def z_in(layer, p, k):
        here = landing(layer, p, slot(k))
        return rc(here, here, zs.at[layer, p, k - 1], zr.at[layer, p, k - 1], (e, slot(k)))

    def own(layer, p):
        return pltpu.make_async_copy(
            cut(layer, p, t), landing(layer, p, t), own_sem.at[layer, p]
        )

    def own_whole(i):
        return pltpu.make_async_copy(ins[i], outs[i].at[e], own_sem.at[0, i])

    def source_of(i, k):
        return outs[i].at[e, slot(k)] if first else ins[i].at[slot(k)]

    def plane(i, k, src, which):
        there = outs[i].at[src, slot(k)]
        dev = ((xn, t), (yn, t))[which]
        source = source_of(i, k) if src is e else there
        return rc(source, there, ps.at[i, k, which], pr.at[i, k, which], dev)

    def diag(i, k, src, which):
        half = outs[i].shape[2] // 2
        there = outs[i].at[src, slot(k), pl.ds(which * half, half)]
        dev = ((yn, t), (xn, t))[which]
        return rc(there, there, ds.at[i, k, which], dr.at[i, k, which], dev)

    def cross(i, k, src, which):
        there = outs[i].at[src, slot(k)]
        source = source_of(i, k) if src is e else there
        return rc(source, there, cs.at[i, k, which], cr.at[i, k, which], (sib, t))

    def parts_of(i):
        return [p for p in range(len(parts)) if parts[p][0] == i]

    def stage0(i, k):
        for p in parts_of(i):
            if k > 0:
                z_in(0, p, k).wait_recv()
            else:
                own(0, p).wait()
        plane(i, k, e, 0).start()
        plane(i, k, e, 1).start()
        cross(i, k, e, 0).start()

    def stage1(i, k):
        plane(i, k, xn, 0).wait_recv()
        diag(i, k, xn, 0).start()
        cross(i, k, xn, 1).start()
        plane(i, k, yn, 1).wait_recv()
        diag(i, k, yn, 1).start()
        cross(i, k, yn, 2).start()

    def stage2(i, k):
        diag(i, k, dg, 0).wait_recv()
        diag(i, k, dg, 1).wait_recv()
        cross(i, k, dg, 3).start()

    def stage3(i, k):
        sx, sy = xn + sib - e, yn + sib - e
        for which, src in enumerate((sib, sx, sy, sx + sy - sib)):
            cross(i, k, src, which).wait_recv()
        plane(i, k, e, 0).wait_send()
        plane(i, k, e, 1).wait_send()
        diag(i, k, xn, 0).wait_send()
        diag(i, k, yn, 1).wait_send()
        for which, src in enumerate((e, xn, yn, dg)):
            cross(i, k, src, which).wait_send()

    is_end = (t == 0) | (t == TENSORS - 1)
    end_peer = jnp.where(t < 2, 1 - t, 5 - t)
    mid_peer = 3 - t

    def band(ref, c):
        size = ref.shape[0] // SUM_CHUNKS
        return ref.at[pl.ds(c * size, size)]

    def end_copy(c):
        return rc(band(term, c), band(got_end, c), e_send.at[c], e_recv.at[c], (e, end_peer))

    def mid_copy(c):
        return rc(band(mine, c), band(got_mid, c), m_send.at[c], m_recv.at[c], (e, mid_peer))

    def out_copy(c):
        return rc(band(total, c), band(total, c), o_send.at[c], o_recv.at[c], (e, end_peer))

    def wide(ref, c):
        return band(ref, c)[...].astype(jnp.float32)

    def mid_first(c):
        end_copy(c).wait_recv()
        band(mine, c)[...] = (wide(term, c) + wide(got_end, c)).astype(jnp.bfloat16)
        mid_copy(c).start()

    def mid_second(c):
        mid_copy(c).wait_recv()
        both = wide(mine, c) + wide(got_mid, c)
        band(total, c)[...] = (wide(resid, c) + both).astype(jnp.bfloat16)
        out_copy(c).start()

    def sum_steps(low, high):
        def each(start, stop, body):
            start, stop = max(low, start), min(high, stop)
            if start < stop:

                @pl.loop(start, stop)
                def _(c):
                    body(c)

        @pl.when(is_end)
        def _():
            each(0, WINDOW, lambda c: end_copy(c).start())

            def later(c):
                end_copy(c - WINDOW).wait_send()
                end_copy(c).start()

            each(WINDOW, SUM_CHUNKS, later)

        @pl.when(jnp.logical_not(is_end))
        def _():
            each(0, LAG, mid_first)

            def both(c):
                mid_first(c)
                mid_second(c - LAG)

            each(LAG, SUM_CHUNKS, both)
            each(SUM_CHUNKS, SUM_CHUNKS + LAG, lambda c: mid_second(c - LAG))

    order = [(i, k) for i in range(n_outs) for k in range(TENSORS)]
    offsets = range(1, TENSORS)
    z_plan = {}
    if first:
        for layer in range(2):
            for p in range(len(parts)):
                own(layer, p).start()
        early = [(0, p, k) for k in offsets for p in parts_of(0)]
        rest = [(layer, p, k) for layer in range(2) for i in range(n_outs) for k in offsets
                for p in parts_of(i) if layer or i]
        for item in early:
            z_out(*item).start()
        for n, item in enumerate(rest):
            z_plan.setdefault(1 + n * (len(order) - 2) // len(rest), []).append(item)
    elif n_outs:
        for i in range(n_outs):
            own_whole(i).start()
    all_sums = SUM_CHUNKS + LAG
    if with_sum and not n_outs:
        sum_steps(0, all_sums)
    if n_outs:
        steps = len(order) + 2
        for step in range(steps):
            if step < len(order):
                stage0(*order[step])
                for item in z_plan.get(step, []):
                    z_out(*item).start()
            if with_sum:
                sum_steps(all_sums * step // steps, all_sums * (step + 1) // steps)
            if 0 <= step - 1 < len(order):
                stage1(*order[step - 1])
            if 0 <= step - 2 < len(order):
                stage2(*order[step - 2])
        for item in order:
            stage3(*item)
    if first:
        for p in range(len(parts)):
            own(1, p).wait()
            for k in offsets:
                z_out(0, p, k).wait_send()
                z_in(1, p, k).wait_recv()
                z_out(1, p, k).wait_send()
    elif n_outs:
        for i in range(n_outs):
            own_whole(i).wait()
    if with_sum:

        @pl.when(is_end)
        def _():
            @pl.loop(SUM_CHUNKS - WINDOW, SUM_CHUNKS)
            def _(c):
                end_copy(c).wait_send()

            @pl.loop(0, SUM_CHUNKS)
            def _(c):
                out_copy(c).wait_recv()

        @pl.when(jnp.logical_not(is_end))
        def _():
            @pl.loop(0, SUM_CHUNKS)
            def _(c):
                mid_copy(c).wait_send()
                out_copy(c).wait_send()


def communicate(sources, parts, blocks, sums, collective_id):
    n = len(blocks)
    dma = pltpu.SemaphoreType.DMA
    outs = [jax.ShapeDtypeStruct((ENGINES, TENSORS) + b, jnp.bfloat16) for b in blocks]
    if parts:
        outs += [jax.ShapeDtypeStruct((TENSORS,) + b, jnp.bfloat16) for b in blocks]
    in_specs = [pl.BlockSpec(memory_space=pl.ANY)] * len(sources)
    out_specs = [pl.BlockSpec(memory_space=pl.ANY)] * len(outs)
    scratch = []
    if n:
        scratch += [dma((2, max(n, len(parts))))] + [dma((n, TENSORS, 2))] * 4
        scratch += [dma((n, TENSORS, 4))] * 2
    if parts:
        scratch += [dma((2, len(parts), TENSORS - 1))] * 2
    if sums:
        in_specs += [pl.BlockSpec(memory_space=pltpu.VMEM)] * 2
        outs.append(jax.ShapeDtypeStruct(sums[0].shape, jnp.bfloat16))
        out_specs.append(pl.BlockSpec(memory_space=pltpu.VMEM))
        scratch += [pltpu.VMEM(sums[0].shape, jnp.bfloat16)] * 3
        scratch += [dma((SUM_CHUNKS,))] * 6
    return pl.pallas_call(
        functools.partial(comm_kernel, parts, n, bool(sums)),
        out_shape=outs,
        in_specs=in_specs,
        out_specs=out_specs,
        scratch_shapes=scratch,
        compiler_params=pltpu.CompilerParams(
            collective_id=collective_id, has_side_effects=True, vmem_limit_bytes=44 * 1024 * 1024
        ),
        cost_estimate=pl.CostEstimate(flops=0, bytes_accessed=60_000_000, transcendentals=0),
    )(*sources, *sums)


def attention_kernel(heads, keys, proj, cosine, sine_part, gain, allowed, attended, cache):
    rows = proj.shape[0]
    size = gain.shape[1]
    block = rows // 2

    def normed_rotated(low, high, column, which):
        values = proj[low:high, column : column + size]
        values = values * lax.rsqrt(jnp.mean(values * values, axis=-1, keepdims=True) + EPS)
        values = values * gain[which : which + 1, :]
        turned = values * cosine[low:high, :]
        turned += pltpu.roll(values, size // 2, 1) * sine_part[low:high, :]
        return turned.astype(jnp.bfloat16)

    for key in range(keys):
        column = heads * size + key * 2 * size
        cache[:, key * 2 * size : key * 2 * size + size] = normed_rotated(0, rows, column, 1)
        cache[:, key * 2 * size + size : (key + 1) * 2 * size] = proj[
            :, column + size : column + 2 * size
        ].astype(jnp.bfloat16)
    for head in range(heads):
        base = head // (heads // keys) * 2 * size
        for low in range(0, rows, block):
            high = low + block
            queries = normed_rotated(low, high, head * size, 0)
            scores = lax.dot_general(
                queries,
                cache[0:high, base : base + size],
                (((1,), (1,)), ((), ())),
                preferred_element_type=jnp.float32,
            ) * size ** (-0.5)
            raised = jnp.exp(scores) * allowed[low:high, 0:high]
            share = 1.0 / jnp.sum(raised, axis=-1, keepdims=True)
            weights = (raised * share).astype(jnp.bfloat16)
            attended[low:high, head * size : (head + 1) * size] = jnp.dot(
                weights,
                cache[0:high, base + size : base + 2 * size],
                preferred_element_type=jnp.float32,
            ).astype(jnp.bfloat16)


def attention(projected, cosine, sine_part, gain, allowed, heads, keys):
    rows, size = projected.shape[0], gain.shape[-1]
    return pl.pallas_call(
        functools.partial(attention_kernel, heads, keys),
        out_shape=[
            jax.ShapeDtypeStruct((rows, heads * size), jnp.bfloat16),
            jax.ShapeDtypeStruct((rows, keys * 2 * size), jnp.bfloat16),
        ],
        in_specs=[pl.BlockSpec(memory_space=pltpu.VMEM)] * 5,
        out_specs=[pl.BlockSpec(memory_space=pltpu.VMEM)] * 2,
        compiler_params=pltpu.CompilerParams(vmem_limit_bytes=40 * 1024 * 1024),
    )(projected, cosine, sine_part, gain, allowed)


def fast_shards(hidden, lengths, assignment, wq, wkv, wo, norm_gain, qk_gain):
    row_count, width = hidden.shape
    head_size = qk_gain.shape[-1]
    layer_total, depth = wq.shape[0], wq.shape[1]
    q_width, kv_width = wq.shape[2] // TENSORS, wkv.shape[2] // TENSORS
    heads, keys = q_width // head_size, kv_width // (2 * head_size)
    segment, position = row_layout(lengths, assignment, lax.axis_index("engine"), row_count)
    cosine, sine_part = rope_tables(position, head_size)
    cosine = jnp.concatenate([cosine[:, 0], cosine[:, 0]], axis=1)
    sine_part = jnp.concatenate([-sine_part[:, 0], sine_part[:, 0]], axis=1)
    row_ids = jnp.arange(row_count, dtype=jnp.int32)
    allowed = (segment[:, None] == segment[None, :]) & (row_ids[None, :] <= row_ids[:, None])
    allowed = allowed.astype(jnp.float32)

    residual = hidden
    caches = []
    parts = ((0, 0, q_width), (0, q_width, kv_width), (1, 0, q_width))
    blocks = [(depth, q_width + kv_width), (depth, q_width)]
    *weights, staged_qkv, staged_out = communicate(
        [wq, wkv, wo.transpose(0, 2, 1)], parts, blocks, [], 1
    )
    for layer_number in range(layer_total):
        normed = norm_rows(residual, norm_gain[layer_number])
        qkv_weight = weights[0].reshape(width, q_width + kv_width)
        out_weight = weights[1].reshape(width, q_width)
        projected = jnp.dot(normed, qkv_weight, preferred_element_type=jnp.float32)
        attended, cache = attention(
            projected, cosine, sine_part, qk_gain[layer_number], allowed, heads, keys
        )
        caches.append(cache)
        term = lax.dot_general(
            attended, out_weight, (((1,), (1,)), ((), ())), preferred_element_type=jnp.float32
        ).astype(jnp.bfloat16)
        if layer_number + 1 < layer_total:
            *weights, residual = communicate(
                [staged_qkv, staged_out], (), blocks, [term, residual], 2
            )
        else:
            (residual,) = communicate([], (), [], [term, residual], 3)
    return (residual, jnp.stack(caches))


def solution(mesh):
    fits = mesh.shape["engine"] == ENGINES and mesh.shape["tensor"] == TENSORS
    return jax.shard_map(
        fast_shards if fits else shards,
        mesh=mesh,
        in_specs=(
            P("engine", None),
            P(),
            P(),
            P(None, ("engine", "tensor"), None),
            P(None, ("engine", "tensor"), None),
            P(None, None, ("engine", "tensor")),
            P(),
            P(),
        ),
        out_specs=(P("engine", None), P(None, "engine", "tensor")),
        check_vma=False,
    )
```

```python
import functools

import jax
import jax.numpy as jnp
from jax import lax
from jax.experimental import pallas as pl
from jax.experimental.pallas import tpu as pltpu
from jax.sharding import PartitionSpec as P

EPS = 1e-06
THETA = 1000000.0


def row_layout(lengths, assignment, engine, row_count):
    on_engine = assignment == engine
    own_sizes = jnp.where(on_engine, lengths, 0)
    offsets = jnp.cumsum(own_sizes) - own_sizes
    row_ids = jnp.arange(row_count, dtype=jnp.int32)
    inside = (
        on_engine[None, :]
        & (row_ids[:, None] >= offsets[None, :])
        & (row_ids[:, None] < (offsets + own_sizes)[None, :])
    )
    inside_int = inside.astype(jnp.int32)
    seq_index = jnp.arange(lengths.shape[0], dtype=jnp.int32)
    live_count = jnp.sum(inside_int, axis=1)
    segment = jnp.sum(inside_int * seq_index[None, :], axis=1)
    segment = jnp.where(live_count > 0, segment, lengths.shape[0] + row_ids)
    position = row_ids - jnp.sum(inside_int * offsets[None, :], axis=1)
    position = jnp.where(live_count > 0, position, 0)
    return (segment, position)


def rope_tables(position, head_size):
    half_width = head_size // 2
    frequency = jnp.power(
        jnp.float32(THETA), -(jnp.arange(half_width, dtype=jnp.float32) * 2.0 / head_size)
    )
    angles = position.astype(jnp.float32)[:, None] * frequency[None, :]
    return (jnp.cos(angles)[:, None, :], jnp.sin(angles)[:, None, :])


def rotate(values, cosine, sine_part):
    half_width = values.shape[-1] // 2
    first_half = values[..., :half_width]
    second_half = values[..., half_width:]
    return jnp.concatenate(
        [
            first_half * cosine - second_half * sine_part,
            second_half * cosine + first_half * sine_part,
        ],
        axis=-1,
    )


def head_norm(values, gain_row):
    return values * lax.rsqrt(jnp.mean(values * values, axis=-1, keepdims=True) + EPS) * gain_row


def norm_rows(values, gain_row):
    widened = values.astype(jnp.float32)
    return (
        widened * lax.rsqrt(jnp.mean(widened * widened, axis=-1, keepdims=True) + EPS) * gain_row
    ).astype(jnp.bfloat16)


def attend(queries, key_heads, value_heads, segment):
    row_count = queries.shape[0]
    scores = jnp.einsum(
        "rkgd,ckd->kgrc", queries, key_heads, preferred_element_type=jnp.float32
    ) * queries.shape[-1] ** (-0.5)
    row_ids = jnp.arange(row_count, dtype=jnp.int32)
    allowed = (segment[:, None] == segment[None, :]) & (row_ids[None, :] <= row_ids[:, None])
    raised = jnp.exp(scores) * allowed.astype(jnp.float32)
    weights = (raised / jnp.sum(raised, axis=-1, keepdims=True)).astype(jnp.bfloat16)
    attended = jnp.einsum(
        "kgrc,ckd->rkgd", weights, value_heads, preferred_element_type=jnp.float32
    )
    return attended.astype(jnp.bfloat16).reshape(row_count, -1)


def shards(hidden, lengths, assignment, wq, wkv, wo, norm_gain, qk_gain):
    row_count = hidden.shape[0]
    tensor_size = lax.axis_size("tensor")
    head_size = qk_gain.shape[-1]
    layer_total = wq.shape[0]
    local_queries = wq.shape[2] // tensor_size // head_size
    local_keys = wkv.shape[2] // tensor_size // (2 * head_size)
    segment, position = row_layout(lengths, assignment, lax.axis_index("engine"), row_count)
    cosine, sine_part = rope_tables(position, head_size)
    residual = hidden
    normed = norm_rows(hidden, norm_gain[0])
    caches = []
    for layer_number in range(layer_total):
        if layer_number > 0:
            normed = norm_rows(residual, norm_gain[layer_number])
        query_part, keyval_part = (
            lax.all_to_all(wq[layer_number], "tensor", split_axis=1, concat_axis=0, tiled=True),
            lax.all_to_all(wkv[layer_number], "tensor", split_axis=1, concat_axis=0, tiled=True),
        )
        query_weight, keyval_weight = (
            lax.all_gather(query_part, "engine", axis=0, tiled=True),
            lax.all_gather(keyval_part, "engine", axis=0, tiled=True),
        )
        queries = jnp.dot(normed, query_weight, preferred_element_type=jnp.float32)
        keyvals = jnp.dot(normed, keyval_weight, preferred_element_type=jnp.float32)
        queries = queries.reshape(row_count, local_queries, head_size)
        keyvals = keyvals.reshape(row_count, local_keys, 2, head_size)
        queries = rotate(head_norm(queries, qk_gain[layer_number, 0]), cosine, sine_part).astype(
            jnp.bfloat16
        )
        key_heads = rotate(
            head_norm(keyvals[:, :, 0], qk_gain[layer_number, 1]), cosine, sine_part
        ).astype(jnp.bfloat16)
        value_heads = keyvals[:, :, 1].astype(jnp.bfloat16)
        caches.append(
            jnp.stack([key_heads, value_heads], axis=2).reshape(
                row_count, local_keys * 2 * head_size
            )
        )
        attended = attend(
            queries.reshape(row_count, local_keys, local_queries // local_keys, head_size),
            key_heads,
            value_heads,
            segment,
        )
        out_part = lax.all_to_all(
            wo[layer_number], "tensor", split_axis=0, concat_axis=1, tiled=True
        )
        out_weight = lax.all_gather(out_part, "engine", axis=1, tiled=True)
        partial_term = jnp.dot(attended, out_weight, preferred_element_type=jnp.float32)
        summed = lax.psum(partial_term.astype(jnp.bfloat16), "tensor").astype(jnp.float32)
        residual = (residual.astype(jnp.float32) + summed).astype(jnp.bfloat16)
    return (residual, jnp.stack(caches))


MESH = pl.DeviceIdType.MESH
ENGINES, TENSORS = 8, 4
STRIP, WINDOW, LAG = 256, 4, 2


def comm_kernel(parts, n_outs, with_sum, *refs):
    refs = list(refs)
    first = len(parts) > 0
    n_in = len(parts) if first else (1 + TENSORS if n_outs else 0)
    ins = [refs.pop(0) for _ in range(n_in)]
    if with_sum:
        weight, left, resid = refs.pop(0), refs.pop(0), refs.pop(0)
    outs = [refs.pop(0) for _ in range(n_outs)]
    if first:
        staged = [refs.pop(0)]
    if with_sum:
        total = refs.pop(0)
    if n_outs:
        own_sem, ps, pr, ds, dr, cs, cr = refs[:7]
        refs = refs[7:]
    if first:
        zs, zr = refs[:2]
        refs = refs[2:]
    if with_sum:
        weight_in, term, got_end, got_mid = refs[:4]
        w_sem, e_send, e_recv, m_send, m_recv, o_send, o_recv = refs[4:]
        strips = term.shape[0]

    e, t = lax.axis_index("engine"), lax.axis_index("tensor")
    core, xb, yb = e % 2, (e // 2) % 2, e // 4
    sib, xn, yn = e + 1 - 2 * core, e + 2 - 4 * xb, e + 4 - 8 * yb
    dg = xn + yn - e

    barrier = pltpu.get_barrier_semaphore()
    partners = [(e, (t + k) % TENSORS) for k in range(1, TENSORS)]
    if n_outs:
        partners += [(sib, t), (xn, t), (yn, t)]
    for dev in partners:
        pl.semaphore_signal(barrier, inc=1, device_id=dev, device_id_type=MESH)
    pl.semaphore_wait(barrier, len(partners))

    def rc(src, dst, ss, rs, dev):
        return pltpu.make_async_remote_copy(
            src_ref=src, dst_ref=dst, send_sem=ss, recv_sem=rs, device_id=dev, device_id_type=MESH
        )

    def slot(k):
        return (t + TENSORS - k) % TENSORS

    def landing(layer, p, source):
        out, column, size = parts[p]
        ref = outs[out].at[e, source] if layer == 0 else staged[out].at[source]
        return ref.at[:, pl.ds(column, size)]

    def cut(layer, p, target):
        size = parts[p][2]
        return ins[p].at[layer, :, pl.ds(pl.multiple_of(target * size, 128), size)]

    def z_out(layer, p, k):
        to = (t + k) % TENSORS
        sems = (zs.at[layer, p, k - 1], zr.at[layer, p, k - 1])
        return rc(cut(layer, p, to), landing(layer, p, t), *sems, (e, to))

    def z_in(layer, p, k):
        here = landing(layer, p, slot(k))
        return rc(here, here, zs.at[layer, p, k - 1], zr.at[layer, p, k - 1], (e, slot(k)))

    def own(layer, p):
        return pltpu.make_async_copy(
            cut(layer, p, t), landing(layer, p, t), own_sem.at[layer, p]
        )

    def source_of(i, k):
        if first:
            return outs[i].at[e, slot(k)]
        return ins[0].at[slot(k)] if i == 0 else ins[1 + k]

    def own_later(i, k):
        return pltpu.make_async_copy(source_of(i, k), outs[i].at[e, slot(k)], own_sem.at[i, k])

    def plane(i, k, src, which):
        there = outs[i].at[src, slot(k)]
        dev = ((xn, t), (yn, t))[which]
        source = source_of(i, k) if src is e else there
        return rc(source, there, ps.at[i, k, which], pr.at[i, k, which], dev)

    def diag(i, k, src, which):
        half = outs[i].shape[2] // 2
        there = outs[i].at[src, slot(k), pl.ds(which * half, half)]
        dev = ((yn, t), (xn, t))[which]
        return rc(there, there, ds.at[i, k, which], dr.at[i, k, which], dev)

    def cross(i, k, src, which):
        there = outs[i].at[src, slot(k)]
        source = source_of(i, k) if src is e else there
        return rc(source, there, cs.at[i, k, which], cr.at[i, k, which], (sib, t))

    def parts_of(i):
        return [p for p in range(len(parts)) if parts[p][0] == i]

    def stage0(i, k):
        for p in parts_of(i):
            if k > 0:
                z_in(0, p, k).wait_recv()
            else:
                own(0, p).wait()
        plane(i, k, e, 0).start()
        plane(i, k, e, 1).start()
        cross(i, k, e, 0).start()

    def stage1(i, k):
        plane(i, k, xn, 0).wait_recv()
        diag(i, k, xn, 0).start()
        cross(i, k, xn, 1).start()
        plane(i, k, yn, 1).wait_recv()
        diag(i, k, yn, 1).start()
        cross(i, k, yn, 2).start()

    def stage2(i, k):
        diag(i, k, dg, 0).wait_recv()
        diag(i, k, dg, 1).wait_recv()
        cross(i, k, dg, 3).start()

    def stage3(i, k):
        sx, sy = xn + sib - e, yn + sib - e
        for which, src in enumerate((sib, sx, sy, sx + sy - sib)):
            cross(i, k, src, which).wait_recv()
        plane(i, k, e, 0).wait_send()
        plane(i, k, e, 1).wait_send()
        diag(i, k, xn, 0).wait_send()
        diag(i, k, yn, 1).wait_send()
        for which, src in enumerate((e, xn, yn, dg)):
            cross(i, k, src, which).wait_send()

    is_end = (t == 0) | (t == TENSORS - 1)
    end_peer = jnp.where(t < 2, 1 - t, 5 - t)
    mid_peer = 3 - t

    def columns(ref, c):
        return ref.at[:, pl.ds(pl.multiple_of(c * STRIP, STRIP), STRIP)]

    def weight_copy(c):
        return pltpu.make_async_copy(
            weight.at[pl.ds(pl.multiple_of(c * STRIP, STRIP), STRIP)], weight_in.at[c], w_sem.at[c]
        )

    def end_copy(c):
        return rc(term.at[c], got_end.at[c], e_send.at[c], e_recv.at[c], (e, end_peer))

    def mid_copy(c):
        return rc(term.at[c], got_mid.at[c], m_send.at[c], m_recv.at[c], (e, mid_peer))

    def out_copy(c):
        strip = columns(total, c)
        return rc(strip, strip, o_send.at[c], o_recv.at[c], (e, end_peer))

    def project(c):
        weight_copy(c).wait()
        term[c] = lax.dot_general(
            left[...], weight_in[c], (((1,), (1,)), ((), ())), preferred_element_type=jnp.float32
        ).astype(jnp.bfloat16)

    def mid_first(c):
        project(c)
        end_copy(c).wait_recv()
        term[c] = (term[c].astype(jnp.float32) + got_end[c].astype(jnp.float32)).astype(
            jnp.bfloat16
        )
        mid_copy(c).start()

    def mid_second(c):
        mid_copy(c).wait_recv()
        both = term[c].astype(jnp.float32) + got_mid[c].astype(jnp.float32)
        columns(total, c)[...] = (columns(resid, c)[...].astype(jnp.float32) + both).astype(
            jnp.bfloat16
        )
        out_copy(c).start()

    def sum_steps(low, high):
        def each(start, stop, body):
            start, stop = max(low, start), min(high, stop)
            if start < stop:

                @pl.loop(start, stop)
                def _(c):
                    body(c)

        @pl.when(is_end)
        def _():
            def early(c):
                project(c)
                end_copy(c).start()

            each(0, WINDOW, early)

            def later(c):
                project(c)
                end_copy(c - WINDOW).wait_send()
                end_copy(c).start()

            each(WINDOW, strips, later)

        @pl.when(jnp.logical_not(is_end))
        def _():
            each(0, LAG, mid_first)

            def both(c):
                mid_first(c)
                mid_second(c - LAG)

            each(LAG, strips, both)
            each(strips, strips + LAG, lambda c: mid_second(c - LAG))

    order = [(i, k) for i in range(n_outs) for k in range(TENSORS)]
    offsets = range(1, TENSORS)
    z_plan = {}
    if first:
        for layer in range(2):
            for p in range(len(parts)):
                if layer == 0 or parts[p][0] == 0:
                    own(layer, p).start()
        early = [(0, p, k) for k in offsets for p in parts_of(0)]
        rest = [(0, p, k) for k in offsets for p in parts_of(1)]
        rest += [(1, p, k) for k in offsets for p in parts_of(0)]
        for item in early:
            z_out(*item).start()
        for n, item in enumerate(rest):
            z_plan.setdefault(1 + n * (len(order) - 2) // len(rest), []).append(item)
    elif n_outs:
        for item in order:
            own_later(*item).start()
    if with_sum:
        all_sums = strips + LAG

        @pl.loop(0, strips)
        def _(c):
            weight_copy(c).start()

    if with_sum and not n_outs:
        sum_steps(0, all_sums)
    if n_outs:
        steps = len(order) + 2
        for step in range(steps):
            if step < len(order):
                stage0(*order[step])
                for item in z_plan.get(step, []):
                    z_out(*item).start()
            if with_sum:
                sum_steps(all_sums * step // steps, all_sums * (step + 1) // steps)
            if 0 <= step - 1 < len(order):
                stage1(*order[step - 1])
            if 0 <= step - 2 < len(order):
                stage2(*order[step - 2])
        for item in order:
            stage3(*item)
    if first:
        for p in range(len(parts)):
            for k in offsets:
                z_out(0, p, k).wait_send()
        for p in parts_of(0):
            own(1, p).wait()
            for k in offsets:
                z_in(1, p, k).wait_recv()
                z_out(1, p, k).wait_send()
    elif n_outs:
        for item in order:
            own_later(*item).wait()
    if with_sum:

        @pl.when(is_end)
        def _():
            @pl.loop(strips - WINDOW, strips)
            def _(c):
                end_copy(c).wait_send()

            @pl.loop(0, strips)
            def _(c):
                out_copy(c).wait_recv()

        @pl.when(jnp.logical_not(is_end))
        def _():
            @pl.loop(0, strips)
            def _(c):
                mid_copy(c).wait_send()
                out_copy(c).wait_send()


def communicate(sources, parts, blocks, sums, collective_id):
    n = len(blocks)
    dma = pltpu.SemaphoreType.DMA
    outs = [jax.ShapeDtypeStruct((ENGINES, TENSORS) + b, jnp.bfloat16) for b in blocks]
    if parts:
        outs.append(jax.ShapeDtypeStruct((TENSORS,) + blocks[0], jnp.bfloat16))
    in_specs = [pl.BlockSpec(memory_space=pl.ANY)] * len(sources)
    out_specs = [pl.BlockSpec(memory_space=pl.ANY)] * len(outs)
    scratch = []
    if n:
        scratch += [dma((2, TENSORS))] + [dma((n, TENSORS, 2))] * 4
        scratch += [dma((n, TENSORS, 4))] * 2
    if parts:
        scratch += [dma((2, len(parts), TENSORS - 1))] * 2
    if sums:
        weight, left, resid = sums
        rows, width = resid.shape
        strips = width // STRIP
        in_specs += [pl.BlockSpec(memory_space=pl.ANY)]
        in_specs += [pl.BlockSpec(memory_space=pltpu.VMEM)] * 2
        outs.append(jax.ShapeDtypeStruct(resid.shape, jnp.bfloat16))
        out_specs.append(pl.BlockSpec(memory_space=pltpu.VMEM))
        scratch += [pltpu.VMEM((strips, STRIP, left.shape[1]), jnp.bfloat16)]
        scratch += [pltpu.VMEM((strips, rows, STRIP), jnp.bfloat16)] * 3
        scratch += [dma((strips,))] * 7
    return pl.pallas_call(
        functools.partial(comm_kernel, parts, n, bool(sums)),
        out_shape=outs,
        in_specs=in_specs,
        out_specs=out_specs,
        scratch_shapes=scratch,
        compiler_params=pltpu.CompilerParams(
            collective_id=collective_id, has_side_effects=True, vmem_limit_bytes=50 * 1024 * 1024
        ),
        cost_estimate=pl.CostEstimate(flops=0, bytes_accessed=60_000_000, transcendentals=0),
    )(*sources, *sums)


def attention_kernel(heads, keys, proj, cosine, sine_part, gain, allowed, attended, cache):
    rows = proj.shape[0]
    size = gain.shape[1]
    block = rows // 2

    def normed_rotated(low, high, column, which):
        values = proj[low:high, column : column + size]
        values = values * lax.rsqrt(jnp.mean(values * values, axis=-1, keepdims=True) + EPS)
        values = values * gain[which : which + 1, :]
        turned = values * cosine[low:high, :]
        turned += pltpu.roll(values, size // 2, 1) * sine_part[low:high, :]
        return turned.astype(jnp.bfloat16)

    for key in range(keys):
        column = heads * size + key * 2 * size
        cache[:, key * 2 * size : key * 2 * size + size] = normed_rotated(0, rows, column, 1)
        cache[:, key * 2 * size + size : (key + 1) * 2 * size] = proj[
            :, column + size : column + 2 * size
        ].astype(jnp.bfloat16)
    for head in range(heads):
        base = head // (heads // keys) * 2 * size
        for low in range(0, rows, block):
            high = low + block
            queries = normed_rotated(low, high, head * size, 0)
            scores = lax.dot_general(
                queries,
                cache[0:high, base : base + size],
                (((1,), (1,)), ((), ())),
                preferred_element_type=jnp.float32,
            ) * size ** (-0.5)
            raised = jnp.exp(scores) * allowed[low:high, 0:high]
            share = 1.0 / jnp.sum(raised, axis=-1, keepdims=True)
            weights = (raised * share).astype(jnp.bfloat16)
            attended[low:high, head * size : (head + 1) * size] = jnp.dot(
                weights,
                cache[0:high, base + size : base + 2 * size],
                preferred_element_type=jnp.float32,
            ).astype(jnp.bfloat16)


def attention(projected, cosine, sine_part, gain, allowed, heads, keys):
    rows, size = projected.shape[0], gain.shape[-1]
    return pl.pallas_call(
        functools.partial(attention_kernel, heads, keys),
        out_shape=[
            jax.ShapeDtypeStruct((rows, heads * size), jnp.bfloat16),
            jax.ShapeDtypeStruct((rows, keys * 2 * size), jnp.bfloat16),
        ],
        in_specs=[pl.BlockSpec(memory_space=pltpu.VMEM)] * 5,
        out_specs=[pl.BlockSpec(memory_space=pltpu.VMEM)] * 2,
        compiler_params=pltpu.CompilerParams(vmem_limit_bytes=40 * 1024 * 1024),
        cost_estimate=pl.CostEstimate(
            flops=4 * heads * rows * rows * size,
            bytes_accessed=projected.size * 8,
            transcendentals=heads * rows * rows,
        ),
    )(projected, cosine, sine_part, gain, allowed)


def fast_shards(hidden, lengths, assignment, wq, wkv, wo, norm_gain, qk_gain):
    row_count, width = hidden.shape
    head_size = qk_gain.shape[-1]
    layer_total, depth = wq.shape[0], wq.shape[1]
    q_width, kv_width = wq.shape[2] // TENSORS, wkv.shape[2] // TENSORS
    heads, keys = q_width // head_size, kv_width // (2 * head_size)
    segment, position = row_layout(lengths, assignment, lax.axis_index("engine"), row_count)
    cosine, sine_part = rope_tables(position, head_size)
    cosine = jnp.concatenate([cosine[:, 0], cosine[:, 0]], axis=1)
    sine_part = jnp.concatenate([-sine_part[:, 0], sine_part[:, 0]], axis=1)
    row_ids = jnp.arange(row_count, dtype=jnp.int32)
    allowed = (segment[:, None] == segment[None, :]) & (row_ids[None, :] <= row_ids[:, None])
    allowed = allowed.astype(jnp.float32)

    residual = hidden
    caches = []
    parts = ((0, 0, q_width), (0, q_width, kv_width), (1, 0, q_width))
    blocks = [(depth, q_width + kv_width), (depth, q_width)]
    turned = wo.transpose(0, 2, 1)
    *weights, staged = communicate([wq, wkv, turned], parts, blocks, [], 1)
    staged, last = lax.optimization_barrier((staged, turned[1]))
    place = lax.axis_index("tensor")
    sources = [staged]
    for k in range(TENSORS):
        begin = (place + k) % TENSORS * q_width
        piece = lax.dynamic_slice(last, (0, begin), (depth, q_width))
        if k > 0:
            piece = lax.ppermute(piece, "tensor", [(i, (i + k) % TENSORS) for i in range(TENSORS)])
        sources.append(piece)
    for layer_number in range(layer_total):
        normed = norm_rows(residual, norm_gain[layer_number])
        qkv_weight = weights[0].reshape(width, q_width + kv_width)
        out_weight = weights[1].reshape(width, q_width)
        projected = jnp.dot(normed, qkv_weight, preferred_element_type=jnp.float32)
        attended, cache = attention(
            projected, cosine, sine_part, qk_gain[layer_number], allowed, heads, keys
        )
        caches.append(cache)
        sums = [out_weight, attended, residual]
        if layer_number + 1 < layer_total:
            *weights, residual = communicate(sources, (), blocks, sums, 2)
        else:
            (residual,) = communicate([], (), [], sums, 3)
    return (residual, jnp.stack(caches))


def solution(mesh):
    fits = mesh.shape["engine"] == ENGINES and mesh.shape["tensor"] == TENSORS
    return jax.shard_map(
        fast_shards if fits else shards,
        mesh=mesh,
        in_specs=(
            P("engine", None),
            P(),
            P(),
            P(None, ("engine", "tensor"), None),
            P(None, ("engine", "tensor"), None),
            P(None, None, ("engine", "tensor")),
            P(),
            P(),
        ),
        out_specs=(P("engine", None), P(None, "engine", "tensor")),
        check_vma=False,
    )
```

```python
import functools

import jax
import jax.numpy as jnp
from jax import lax
from jax.experimental import pallas as pl
from jax.experimental.pallas import tpu as pltpu
from jax.sharding import PartitionSpec as P

EPS = 1e-06
THETA = 1000000.0


def row_layout(lengths, assignment, engine, row_count):
    on_engine = assignment == engine
    own_sizes = jnp.where(on_engine, lengths, 0)
    offsets = jnp.cumsum(own_sizes) - own_sizes
    row_ids = jnp.arange(row_count, dtype=jnp.int32)
    inside = (
        on_engine[None, :]
        & (row_ids[:, None] >= offsets[None, :])
        & (row_ids[:, None] < (offsets + own_sizes)[None, :])
    )
    inside_int = inside.astype(jnp.int32)
    seq_index = jnp.arange(lengths.shape[0], dtype=jnp.int32)
    live_count = jnp.sum(inside_int, axis=1)
    segment = jnp.sum(inside_int * seq_index[None, :], axis=1)
    segment = jnp.where(live_count > 0, segment, lengths.shape[0] + row_ids)
    position = row_ids - jnp.sum(inside_int * offsets[None, :], axis=1)
    position = jnp.where(live_count > 0, position, 0)
    return (segment, position)


def rope_tables(position, head_size):
    half_width = head_size // 2
    frequency = jnp.power(
        jnp.float32(THETA), -(jnp.arange(half_width, dtype=jnp.float32) * 2.0 / head_size)
    )
    angles = position.astype(jnp.float32)[:, None] * frequency[None, :]
    return (jnp.cos(angles)[:, None, :], jnp.sin(angles)[:, None, :])


def rotate(values, cosine, sine_part):
    half_width = values.shape[-1] // 2
    first_half = values[..., :half_width]
    second_half = values[..., half_width:]
    return jnp.concatenate(
        [
            first_half * cosine - second_half * sine_part,
            second_half * cosine + first_half * sine_part,
        ],
        axis=-1,
    )


def head_norm(values, gain_row):
    return values * lax.rsqrt(jnp.mean(values * values, axis=-1, keepdims=True) + EPS) * gain_row


def norm_rows(values, gain_row):
    widened = values.astype(jnp.float32)
    return (
        widened * lax.rsqrt(jnp.mean(widened * widened, axis=-1, keepdims=True) + EPS) * gain_row
    ).astype(jnp.bfloat16)


def attend(queries, key_heads, value_heads, segment):
    row_count = queries.shape[0]
    scores = jnp.einsum(
        "rkgd,ckd->kgrc", queries, key_heads, preferred_element_type=jnp.float32
    ) * queries.shape[-1] ** (-0.5)
    row_ids = jnp.arange(row_count, dtype=jnp.int32)
    allowed = (segment[:, None] == segment[None, :]) & (row_ids[None, :] <= row_ids[:, None])
    raised = jnp.exp(scores) * allowed.astype(jnp.float32)
    weights = (raised / jnp.sum(raised, axis=-1, keepdims=True)).astype(jnp.bfloat16)
    attended = jnp.einsum(
        "kgrc,ckd->rkgd", weights, value_heads, preferred_element_type=jnp.float32
    )
    return attended.astype(jnp.bfloat16).reshape(row_count, -1)


def shards(hidden, lengths, assignment, wq, wkv, wo, norm_gain, qk_gain):
    row_count = hidden.shape[0]
    tensor_size = lax.axis_size("tensor")
    head_size = qk_gain.shape[-1]
    layer_total = wq.shape[0]
    local_queries = wq.shape[2] // tensor_size // head_size
    local_keys = wkv.shape[2] // tensor_size // (2 * head_size)
    segment, position = row_layout(lengths, assignment, lax.axis_index("engine"), row_count)
    cosine, sine_part = rope_tables(position, head_size)
    residual = hidden
    normed = norm_rows(hidden, norm_gain[0])
    caches = []
    for layer_number in range(layer_total):
        if layer_number > 0:
            normed = norm_rows(residual, norm_gain[layer_number])
        query_part, keyval_part = (
            lax.all_to_all(wq[layer_number], "tensor", split_axis=1, concat_axis=0, tiled=True),
            lax.all_to_all(wkv[layer_number], "tensor", split_axis=1, concat_axis=0, tiled=True),
        )
        query_weight, keyval_weight = (
            lax.all_gather(query_part, "engine", axis=0, tiled=True),
            lax.all_gather(keyval_part, "engine", axis=0, tiled=True),
        )
        queries = jnp.dot(normed, query_weight, preferred_element_type=jnp.float32)
        keyvals = jnp.dot(normed, keyval_weight, preferred_element_type=jnp.float32)
        queries = queries.reshape(row_count, local_queries, head_size)
        keyvals = keyvals.reshape(row_count, local_keys, 2, head_size)
        queries = rotate(head_norm(queries, qk_gain[layer_number, 0]), cosine, sine_part).astype(
            jnp.bfloat16
        )
        key_heads = rotate(
            head_norm(keyvals[:, :, 0], qk_gain[layer_number, 1]), cosine, sine_part
        ).astype(jnp.bfloat16)
        value_heads = keyvals[:, :, 1].astype(jnp.bfloat16)
        caches.append(
            jnp.stack([key_heads, value_heads], axis=2).reshape(
                row_count, local_keys * 2 * head_size
            )
        )
        attended = attend(
            queries.reshape(row_count, local_keys, local_queries // local_keys, head_size),
            key_heads,
            value_heads,
            segment,
        )
        out_part = lax.all_to_all(
            wo[layer_number], "tensor", split_axis=0, concat_axis=1, tiled=True
        )
        out_weight = lax.all_gather(out_part, "engine", axis=1, tiled=True)
        partial_term = jnp.dot(attended, out_weight, preferred_element_type=jnp.float32)
        summed = lax.psum(partial_term.astype(jnp.bfloat16), "tensor").astype(jnp.float32)
        residual = (residual.astype(jnp.float32) + summed).astype(jnp.bfloat16)
    return (residual, jnp.stack(caches))


MESH = pl.DeviceIdType.MESH
ENGINES, TENSORS = 8, 4
STRIP, WINDOW, LAG = 128, 4, 1


def partner(place, k):
    return (place, place + 1 - 2 * (place % 2), (place + 2) % 4, 3 - place)[k]


def comm_kernel(parts, n_outs, with_sum, *refs):
    refs = list(refs)
    first = len(parts) > 0
    n_in = len(parts) if first else (1 + TENSORS if n_outs else 0)
    ins = [refs.pop(0) for _ in range(n_in)]
    if with_sum:
        weight, left, resid = refs.pop(0), refs.pop(0), refs.pop(0)
    outs = [refs.pop(0) for _ in range(n_outs)]
    if first:
        staged = [refs.pop(0)]
    if with_sum:
        total = refs.pop(0)
    if n_outs:
        own_sem, ps, pr, ds, dr, cs, cr = refs[:7]
        refs = refs[7:]
    if first:
        zs, zr = refs[:2]
        refs = refs[2:]
    if with_sum:
        weight_in, term, got_end, got_mid = refs[:4]
        w_sem, e_send, e_recv, m_send, m_recv, o_send, o_recv = refs[4:]
        strips = term.shape[0]

    e, t = lax.axis_index("engine"), lax.axis_index("tensor")
    core, xb, yb = e % 2, (e // 2) % 2, e // 4
    sib, xn, yn = e + 1 - 2 * core, e + 2 - 4 * xb, e + 4 - 8 * yb
    dg = xn + yn - e

    barrier = pltpu.get_barrier_semaphore()
    partners = [(e, (t + k) % TENSORS) for k in range(1, TENSORS)]
    if n_outs:
        partners += [(sib, t), (xn, t), (yn, t)]
    for dev in partners:
        pl.semaphore_signal(barrier, inc=1, device_id=dev, device_id_type=MESH)
    pl.semaphore_wait(barrier, len(partners))

    def rc(src, dst, ss, rs, dev):
        return pltpu.make_async_remote_copy(
            src_ref=src, dst_ref=dst, send_sem=ss, recv_sem=rs, device_id=dev, device_id_type=MESH
        )

    def slot(k):
        return partner(t, k)

    def landing(layer, p, source):
        out, column, size = parts[p]
        ref = outs[out].at[e, source] if layer == 0 else staged[out].at[source]
        return ref.at[:, pl.ds(column, size)]

    def cut(layer, p, target):
        size = parts[p][2]
        return ins[p].at[layer, :, pl.ds(pl.multiple_of(target * size, 128), size)]

    def z_out(layer, p, k):
        to = partner(t, k)
        sems = (zs.at[layer, p, k - 1], zr.at[layer, p, k - 1])
        return rc(cut(layer, p, to), landing(layer, p, t), *sems, (e, to))

    def z_in(layer, p, k):
        here = landing(layer, p, slot(k))
        return rc(here, here, zs.at[layer, p, k - 1], zr.at[layer, p, k - 1], (e, slot(k)))

    def own(layer, p):
        return pltpu.make_async_copy(
            cut(layer, p, t), landing(layer, p, t), own_sem.at[layer, p]
        )

    def source_of(i, k):
        if first:
            return outs[i].at[e, slot(k)]
        return ins[0].at[slot(k)] if i == 0 else ins[1 + k]

    def own_later(i, k):
        return pltpu.make_async_copy(source_of(i, k), outs[i].at[e, slot(k)], own_sem.at[i, k])

    def plane(i, k, src, which):
        there = outs[i].at[src, slot(k)]
        dev = ((xn, t), (yn, t))[which]
        source = source_of(i, k) if src is e else there
        return rc(source, there, ps.at[i, k, which], pr.at[i, k, which], dev)

    def diag(i, k, src, which):
        half = outs[i].shape[2] // 2
        there = outs[i].at[src, slot(k), pl.ds(which * half, half)]
        dev = ((yn, t), (xn, t))[which]
        return rc(there, there, ds.at[i, k, which], dr.at[i, k, which], dev)

    def cross(i, k, src, which):
        there = outs[i].at[src, slot(k)]
        source = source_of(i, k) if src is e else there
        return rc(source, there, cs.at[i, k, which], cr.at[i, k, which], (sib, t))

    def parts_of(i):
        return [p for p in range(len(parts)) if parts[p][0] == i]

    def stage0(i, k):
        for p in parts_of(i):
            if k > 0:
                z_in(0, p, k).wait_recv()
            else:
                own(0, p).wait()
        plane(i, k, e, 0).start()
        plane(i, k, e, 1).start()
        cross(i, k, e, 0).start()

    def stage1(i, k):
        plane(i, k, xn, 0).wait_recv()
        diag(i, k, xn, 0).start()
        cross(i, k, xn, 1).start()
        plane(i, k, yn, 1).wait_recv()
        diag(i, k, yn, 1).start()
        cross(i, k, yn, 2).start()

    def stage2(i, k):
        diag(i, k, dg, 0).wait_recv()
        diag(i, k, dg, 1).wait_recv()
        cross(i, k, dg, 3).start()

    def stage3(i, k):
        sx, sy = xn + sib - e, yn + sib - e
        for which, src in enumerate((sib, sx, sy, sx + sy - sib)):
            cross(i, k, src, which).wait_recv()
        plane(i, k, e, 0).wait_send()
        plane(i, k, e, 1).wait_send()
        diag(i, k, xn, 0).wait_send()
        diag(i, k, yn, 1).wait_send()
        for which, src in enumerate((e, xn, yn, dg)):
            cross(i, k, src, which).wait_send()

    is_end = (t == 0) | (t == TENSORS - 1)
    end_peer = jnp.where(t < 2, 1 - t, 5 - t)
    mid_peer = 3 - t

    def columns(ref, c):
        return ref.at[:, pl.ds(pl.multiple_of(c * STRIP, STRIP), STRIP)]

    def weight_copy(c):
        return pltpu.make_async_copy(
            weight.at[pl.ds(pl.multiple_of(c * STRIP, STRIP), STRIP)], weight_in.at[c], w_sem.at[c]
        )

    def end_copy(c):
        return rc(term.at[c], got_end.at[c], e_send.at[c], e_recv.at[c], (e, end_peer))

    def mid_copy(c):
        return rc(term.at[c], got_mid.at[c], m_send.at[c], m_recv.at[c], (e, mid_peer))

    def out_copy(c):
        strip = columns(total, c)
        return rc(strip, strip, o_send.at[c], o_recv.at[c], (e, end_peer))

    def project(c):
        weight_copy(c).wait()
        term[c] = lax.dot_general(
            left[...], weight_in[c], (((1,), (1,)), ((), ())), preferred_element_type=jnp.float32
        ).astype(jnp.bfloat16)

    def mid_first(c):
        project(c)
        end_copy(c).wait_recv()
        term[c] = (term[c].astype(jnp.float32) + got_end[c].astype(jnp.float32)).astype(
            jnp.bfloat16
        )
        mid_copy(c).start()

    def mid_second(c):
        mid_copy(c).wait_recv()
        both = term[c].astype(jnp.float32) + got_mid[c].astype(jnp.float32)
        columns(total, c)[...] = (columns(resid, c)[...].astype(jnp.float32) + both).astype(
            jnp.bfloat16
        )
        out_copy(c).start()

    def sum_steps(low, high):
        def each(start, stop, body):
            start, stop = max(low, start), min(high, stop)
            if start < stop:

                @pl.loop(start, stop)
                def _(c):
                    body(c)

        @pl.when(is_end)
        def _():
            def early(c):
                project(c)
                end_copy(c).start()

            each(0, WINDOW, early)

            def later(c):
                project(c)
                end_copy(c - WINDOW).wait_send()
                end_copy(c).start()

            each(WINDOW, strips, later)

        @pl.when(jnp.logical_not(is_end))
        def _():
            each(0, LAG, mid_first)

            def both(c):
                mid_first(c)
                mid_second(c - LAG)

            each(LAG, strips, both)
            each(strips, strips + LAG, lambda c: mid_second(c - LAG))

    order = [(i, k) for i in range(n_outs) for k in range(TENSORS)]
    offsets = (2, 3, 1)
    z_plan = {}
    if first:
        for layer in range(2):
            for p in range(len(parts)):
                if layer == 0 or parts[p][0] == 0:
                    own(layer, p).start()
        early = [(0, p, k) for k in offsets for p in parts_of(0)]
        rest = [(0, p, k) for k in offsets for p in parts_of(1)]
        rest += [(1, p, k) for k in offsets for p in parts_of(0)]
        for item in early:
            z_out(*item).start()
        for n, item in enumerate(rest):
            z_plan.setdefault(1 + n * (len(order) - 2) // len(rest), []).append(item)
    elif n_outs:
        for item in order:
            own_later(*item).start()
    if with_sum:
        all_sums = strips + LAG

        @pl.loop(0, strips)
        def _(c):
            weight_copy(c).start()

    if with_sum and not n_outs:
        sum_steps(0, all_sums)
    if n_outs:
        steps = len(order) + 2
        for step in range(steps):
            if step < len(order):
                stage0(*order[step])
                for item in z_plan.get(step, []):
                    z_out(*item).start()
            if with_sum:
                sum_steps(all_sums * step // steps, all_sums * (step + 1) // steps)
            if 0 <= step - 1 < len(order):
                stage1(*order[step - 1])
            if 0 <= step - 2 < len(order):
                stage2(*order[step - 2])
        for item in order:
            stage3(*item)
    if first:
        for p in range(len(parts)):
            for k in offsets:
                z_out(0, p, k).wait_send()
        for p in parts_of(0):
            own(1, p).wait()
            for k in offsets:
                z_in(1, p, k).wait_recv()
                z_out(1, p, k).wait_send()
    elif n_outs:
        for item in order:
            own_later(*item).wait()
    if with_sum:

        @pl.when(is_end)
        def _():
            @pl.loop(strips - WINDOW, strips)
            def _(c):
                end_copy(c).wait_send()

            @pl.loop(0, strips)
            def _(c):
                out_copy(c).wait_recv()

        @pl.when(jnp.logical_not(is_end))
        def _():
            @pl.loop(0, strips)
            def _(c):
                mid_copy(c).wait_send()
                out_copy(c).wait_send()


def communicate(sources, parts, blocks, sums, collective_id):
    n = len(blocks)
    dma = pltpu.SemaphoreType.DMA
    outs = [jax.ShapeDtypeStruct((ENGINES, TENSORS) + b, jnp.bfloat16) for b in blocks]
    if parts:
        outs.append(jax.ShapeDtypeStruct((TENSORS,) + blocks[0], jnp.bfloat16))
    in_specs = [pl.BlockSpec(memory_space=pl.ANY)] * len(sources)
    out_specs = [pl.BlockSpec(memory_space=pl.ANY)] * len(outs)
    scratch = []
    if n:
        scratch += [dma((2, TENSORS))] + [dma((n, TENSORS, 2))] * 4
        scratch += [dma((n, TENSORS, 4))] * 2
    if parts:
        scratch += [dma((2, len(parts), TENSORS - 1))] * 2
    if sums:
        weight, left, resid = sums
        rows, width = resid.shape
        strips = width // STRIP
        in_specs += [pl.BlockSpec(memory_space=pl.ANY)]
        in_specs += [pl.BlockSpec(memory_space=pltpu.VMEM)] * 2
        outs.append(jax.ShapeDtypeStruct(resid.shape, jnp.bfloat16))
        out_specs.append(pl.BlockSpec(memory_space=pltpu.VMEM))
        scratch += [pltpu.VMEM((strips, STRIP, left.shape[1]), jnp.bfloat16)]
        scratch += [pltpu.VMEM((strips, rows, STRIP), jnp.bfloat16)] * 3
        scratch += [dma((strips,))] * 7
    return pl.pallas_call(
        functools.partial(comm_kernel, parts, n, bool(sums)),
        out_shape=outs,
        in_specs=in_specs,
        out_specs=out_specs,
        scratch_shapes=scratch,
        compiler_params=pltpu.CompilerParams(
            collective_id=collective_id, has_side_effects=True, vmem_limit_bytes=50 * 1024 * 1024
        ),
        cost_estimate=pl.CostEstimate(flops=0, bytes_accessed=60_000_000, transcendentals=0),
    )(*sources, *sums)


def attention_kernel(heads, keys, proj, cosine, sine_part, gain, allowed, attended, cache):
    rows = proj.shape[0]
    size = gain.shape[1]
    block = rows // 2

    def normed_rotated(low, high, column, which):
        values = proj[low:high, column : column + size]
        values = values * lax.rsqrt(jnp.mean(values * values, axis=-1, keepdims=True) + EPS)
        values = values * gain[which : which + 1, :]
        turned = values * cosine[low:high, :]
        turned += pltpu.roll(values, size // 2, 1) * sine_part[low:high, :]
        return turned.astype(jnp.bfloat16)

    for key in range(keys):
        column = heads * size + key * 2 * size
        cache[:, key * 2 * size : key * 2 * size + size] = normed_rotated(0, rows, column, 1)
        cache[:, key * 2 * size + size : (key + 1) * 2 * size] = proj[
            :, column + size : column + 2 * size
        ].astype(jnp.bfloat16)
    for head in range(heads):
        base = head // (heads // keys) * 2 * size
        for low in range(0, rows, block):
            high = low + block
            queries = normed_rotated(low, high, head * size, 0)
            scores = lax.dot_general(
                queries,
                cache[0:high, base : base + size],
                (((1,), (1,)), ((), ())),
                preferred_element_type=jnp.float32,
            ) * size ** (-0.5)
            raised = jnp.exp(scores) * allowed[low:high, 0:high]
            share = 1.0 / jnp.sum(raised, axis=-1, keepdims=True)
            weights = (raised * share).astype(jnp.bfloat16)
            attended[low:high, head * size : (head + 1) * size] = jnp.dot(
                weights,
                cache[0:high, base + size : base + 2 * size],
                preferred_element_type=jnp.float32,
            ).astype(jnp.bfloat16)


def attention(projected, cosine, sine_part, gain, allowed, heads, keys):
    rows, size = projected.shape[0], gain.shape[-1]
    return pl.pallas_call(
        functools.partial(attention_kernel, heads, keys),
        out_shape=[
            jax.ShapeDtypeStruct((rows, heads * size), jnp.bfloat16),
            jax.ShapeDtypeStruct((rows, keys * 2 * size), jnp.bfloat16),
        ],
        in_specs=[pl.BlockSpec(memory_space=pltpu.VMEM)] * 5,
        out_specs=[pl.BlockSpec(memory_space=pltpu.VMEM)] * 2,
        compiler_params=pltpu.CompilerParams(vmem_limit_bytes=40 * 1024 * 1024),
        cost_estimate=pl.CostEstimate(
            flops=4 * heads * rows * rows * size,
            bytes_accessed=projected.size * 8,
            transcendentals=heads * rows * rows,
        ),
    )(projected, cosine, sine_part, gain, allowed)


def fast_shards(hidden, lengths, assignment, wq, wkv, wo, norm_gain, qk_gain):
    row_count, width = hidden.shape
    head_size = qk_gain.shape[-1]
    layer_total, depth = wq.shape[0], wq.shape[1]
    q_width, kv_width = wq.shape[2] // TENSORS, wkv.shape[2] // TENSORS
    heads, keys = q_width // head_size, kv_width // (2 * head_size)
    segment, position = row_layout(lengths, assignment, lax.axis_index("engine"), row_count)
    cosine, sine_part = rope_tables(position, head_size)
    cosine = jnp.concatenate([cosine[:, 0], cosine[:, 0]], axis=1)
    sine_part = jnp.concatenate([-sine_part[:, 0], sine_part[:, 0]], axis=1)
    row_ids = jnp.arange(row_count, dtype=jnp.int32)
    allowed = (segment[:, None] == segment[None, :]) & (row_ids[None, :] <= row_ids[:, None])
    allowed = allowed.astype(jnp.float32)

    residual = hidden
    caches = []
    parts = ((0, 0, q_width), (0, q_width, kv_width), (1, 0, q_width))
    blocks = [(depth, q_width + kv_width), (depth, q_width)]
    turned = wo.transpose(0, 2, 1)
    *weights, staged = communicate([wq, wkv, turned], parts, blocks, [], 1)
    staged, last = lax.optimization_barrier((staged, turned[1]))
    place = lax.axis_index("tensor")
    sources = [staged]
    for k in range(TENSORS):
        begin = partner(place, k) * q_width
        piece = lax.dynamic_slice(last, (0, begin), (depth, q_width))
        if k > 0:
            piece = lax.ppermute(piece, "tensor", [(i, partner(i, k)) for i in range(TENSORS)])
        sources.append(piece)
    for layer_number in range(layer_total):
        normed = norm_rows(residual, norm_gain[layer_number])
        qkv_weight = weights[0].reshape(width, q_width + kv_width)
        out_weight = weights[1].reshape(width, q_width)
        projected = jnp.dot(normed, qkv_weight, preferred_element_type=jnp.float32)
        attended, cache = attention(
            projected, cosine, sine_part, qk_gain[layer_number], allowed, heads, keys
        )
        caches.append(cache)
        sums = [out_weight, attended, residual]
        if layer_number + 1 < layer_total:
            *weights, residual = communicate(sources, (), blocks, sums, 2)
        else:
            (residual,) = communicate([], (), [], sums, 3)
    return (residual, jnp.stack(caches))


def solution(mesh):
    fits = mesh.shape["engine"] == ENGINES and mesh.shape["tensor"] == TENSORS
    return jax.shard_map(
        fast_shards if fits else shards,
        mesh=mesh,
        in_specs=(
            P("engine", None),
            P(),
            P(),
            P(None, ("engine", "tensor"), None),
            P(None, ("engine", "tensor"), None),
            P(None, None, ("engine", "tensor")),
            P(),
            P(),
        ),
        out_specs=(P("engine", None), P(None, "engine", "tensor")),
        check_vma=False,
    )
```
